1024 devices in a mesh: row: 32 (over z_lo, y), col: 32 (over z_hi, x, core).
Axes of the slice: x: 4, y: 4, z: 32 (z_hi: 4, z_lo: 8; z = z_hi * 8 + z_lo), core: 2. Of those that a mesh axis runs over, the one named last changes fastest.
Arguments:
- factor_panel: bfloat16 [32768, 1024], P('row', 'col'), may hold values from -0.03125 to 0.03125
- ancestor_inverse: bfloat16 [32768, 32768], P('row', 'col'), may hold values from -6 to 6
- pattern: int32 [256], replicated, may hold values 0 or 1
- diag_base: float32 [1024], P('col'), may hold values from 0.5 to 2
Outputs:
- offdiag_inverse: bfloat16 [32768, 1024], P('row', 'col')
- diag_inverse: float32 [1024], P('col')
The draws below stay inside these ranges and needn't reach their ends.
All inputs are finite; a program needn't handle non-finite values.
Results may differ from the reference program's by a relative error of at most 0.0044.
Values may be sent and summed in bfloat16 or wider, within the bound.
A program may use at most 32 MiB of HBM per device.

```python
import math
import jax
import jax.numpy as jnp

W = 1024
BLOCK = 128
M = 32768
NBLK = 256


def plant(values, own_key, smallest, top_value):
    dims = values.shape
    spot = [jax.random.randint(jax.random.fold_in(own_key, axis), (), 0, dims[axis]) for axis in range(len(dims))]
    values = values.at[tuple(spot)].set(smallest)
    longest = dims.index(max(dims))
    spot[longest] = (spot[longest] + 1) % dims[longest]
    return values.at[tuple(spot)].set(top_value)


def shard_levels(key, extent, cuts, low, largest):
    def one(dim, shards_of):
        draws = jax.random.uniform(jax.random.fold_in(jax.random.fold_in(key, 6), dim), (shards_of,), jnp.float32, low / len(cuts), largest / len(cuts))
        return jnp.repeat(jnp.exp(draws), extent[dim] // shards_of).reshape((-1,) + (1,) * (len(extent) - dim - 1))

    gain = one(*cuts[0])
    for cut in cuts[1:]:
        gain = gain * one(*cut)
    return gain


def noise(key, extent, spread, most, cuts=(), held_as=jnp.bfloat16):
    factor_of = shard_levels(key, extent, cuts, -0.22, 0.18) if cuts else 1.0
    drawn = jax.random.normal(key, extent, jnp.float32) * spread * factor_of
    return jnp.minimum(jnp.maximum(drawn, -most), most).astype(held_as)


def setup_inputs(seed: int = 0) -> dict:
    keys = jax.random.split(jax.random.key(seed), 5)
    factor_panel = noise(keys[0], (M, W), M ** -0.5, 0.03125, ((0, 32), (1, 32)))
    ancestor_inverse = noise(keys[1], (M, M), 1.0, 6.0, ((0, 32), (1, 32)))
    pattern = plant((jax.random.randint(keys[2], (NBLK,), 0, 4) < 3).astype(jnp.int32), jax.random.fold_in(keys[2], 1), 0, 1)
    diag_base = jnp.clip(jnp.exp(math.log(2.0) - 1.3862944 * jax.random.uniform(keys[3], (W,), jnp.float32) ** shard_levels(keys[3], (W,), ((0, 32),), -0.2, 0.2)), 0.5, 2.0)
    return {"factor_panel": factor_panel, "ancestor_inverse": ancestor_inverse, "pattern": pattern, "diag_base": diag_base}


def reference(factor_panel, ancestor_inverse, pattern, diag_base):
    row_mask = jnp.repeat(pattern.astype(jnp.float32), BLOCK)
    masked = factor_panel * row_mask[:, None].astype(jnp.bfloat16)
    product = jnp.dot(ancestor_inverse, masked, preferred_element_type=jnp.float32)
    offdiag_inverse = (-(row_mask[:, None] * product)).astype(jnp.bfloat16)
    diag_inverse = diag_base + jnp.sum(masked.astype(jnp.float32) * product, axis=0)
    return offdiag_inverse, diag_inverse
```

```python
import functools

import jax
import jax.numpy as jnp
from jax import lax
from jax.experimental import pallas as pl
from jax.experimental.pallas import tpu as pltpu
from jax.sharding import PartitionSpec as P

MESH = pl.DeviceIdType.MESH
BF16 = jnp.bfloat16
F32 = jnp.float32
OFFS = (1, 3, 2, 0)


def aligned(i, n):
    return pl.multiple_of(i * n, n)


def kernel(pattern_ref, f_ref, base_ref, a_hbm, out_ref, diag_ref,
           a_ref, mask_ref, ft_ref, g_ref, p_ref, cs_ref, cr_ref, xs_ref, xr_ref, xo_ref,
           zs_ref, zr_ref, dz_ref, dy_ref,
           a_sem, ts, tr, zs, zr, ys, yr, cs, cr, xs, xr, hs, hr, ds_, dr, es, er):
    r, c = lax.axis_index("row"), lax.axis_index("col")
    zl, y = r // 4, r % 4
    zh, x, k = c // 8, (c // 2) % 4, c % 2
    half, q = zl // 4, zl % 4

    def row_of(zl_, y_):
        return zl_ * 4 + y_

    def col_of(zh_, x_, k_):
        return (zh_ * 4 + x_) * 2 + k_

    barrier = pltpu.get_barrier_semaphore()

    def greet(dev):
        pl.semaphore_signal(barrier, inc=1, device_id=dev, device_id_type=MESH)

    a_copy = pltpu.make_async_copy(a_hbm, a_ref, a_sem)
    a_copy.start()
    for i in range(8):
        src_col = (i // 2 * 4 + y) * 2 + i % 2
        pl.when(jnp.logical_or(c != r, src_col != c))(lambda s=src_col: greet((c, s)))
    for o in range(1, 8):
        greet((row_of((zl + o) % 8, y), c))
    for o in range(1, 4):
        greet((row_of(zl, (y + o) % 4), c))
        greet((r, col_of(zh, (x + o) % 4, k)))
        greet((r, col_of((zh + o) % 4, x, k)))
    greet((r, col_of(zh, x, 1 - k)))

    for b in range(8):
        m = pattern_ref[r * 8 + b].astype(F32)
        mask_ref[:, b * 128:(b + 1) * 128] = jnp.full((32, 128), m, F32)
    ft_ref[...] = (f_ref[...].astype(F32) * mask_ref[...]).astype(BF16)

    self_t = jnp.logical_and(c == r, row_of(zl, x) == r)
    pl.semaphore_wait(barrier, 25 - self_t.astype(jnp.int32))

    pending = []
    t_rows = pl.ds(aligned(c, 32), 32)
    t_copies = []
    for h in range(2):
        for p in range(4):
            lanes = pl.ds(p * 256, 256)
            there = row_of(h * 4 + p, x)
            here = jnp.logical_and(c == r, there == r)
            remote = pltpu.make_async_remote_copy(
                ft_ref.at[:, lanes], g_ref.at[t_rows, lanes], ts.at[h * 4 + p], tr.at[zh * 2 + k],
                device_id=(there, r), device_id_type=MESH)
            local = pltpu.make_async_copy(
                ft_ref.at[:, lanes], g_ref.at[t_rows, lanes], tr.at[zh * 2 + k])
            pl.when(jnp.logical_not(here))(remote.start)
            pl.when(here)(local.start)
            t_copies.append((here, remote))

    def w_of(j):
        return (zh + OFFS[j]) % 4

    q_lanes = pl.ds(aligned(q, 256), 256)

    def z_copies(j):
        rows = pl.ds(aligned(w_of(j) * 4 + y, 64), 64)
        return [pltpu.make_async_remote_copy(
            g_ref.at[rows, q_lanes], g_ref.at[rows, q_lanes], zs.at[j * 3 + o - 1], zr.at[w_of(j) * 3 + o - 1],
            device_id=(row_of(half * 4 + (q + o) % 4, y), c), device_id_type=MESH) for o in range(1, 4)]

    def y_copies(j):
        rows = pl.ds(aligned(w_of(j) * 4 + y, 64), 64)
        return [pltpu.make_async_remote_copy(
            g_ref.at[rows, :], g_ref.at[rows, :], ys.at[j * 3 + o - 1], yr.at[w_of(j) * 3 + o - 1],
            device_id=(row_of(zl, (y + o) % 4), c), device_id_type=MESH) for o in range(1, 4)]

    def core_copy(j):
        return pltpu.make_async_remote_copy(
            cs_ref.at[j], cr_ref.at[j], cs.at[j], cr.at[j],
            device_id=(r, col_of(zh, x, 1 - k)), device_id_type=MESH)

    def x_copies(j):
        return [pltpu.make_async_remote_copy(
            xs_ref.at[j, o - 1], xr_ref.at[j, o - 1], xs.at[j * 3 + o - 1], xr.at[j * 3 + o - 1],
            device_id=(r, col_of(zh, (x + o) % 4, k)), device_id_type=MESH) for o in range(1, 4)]

    def h_copy(o):
        return pltpu.make_async_remote_copy(
            zs_ref.at[o - 1], zr_ref.at[o - 1], hs.at[o - 1], hr.at[o - 1],
            device_id=(r, col_of((zh + o) % 4, x, k)), device_id_type=MESH)

    def send(copies):
        for copy in copies:
            copy.start()
            pending.append(copy)

    def z_stage(j):
        for kk in range(2):
            rows = pl.ds(aligned((w_of(j) * 4 + y) * 2 + kk, 32), 32)
            pltpu.make_async_copy(g_ref.at[rows, q_lanes], g_ref.at[rows, q_lanes], tr.at[w_of(j) * 2 + kk]).wait()
        send(z_copies(j))

    def y_stage(j):
        for copy in z_copies(j):
            copy.wait_recv()
        send(y_copies(j))

    def product_stage(j):
        for copy in y_copies(j):
            copy.wait_recv()
        rows = pl.ds(aligned(w_of(j), 256), 256)

        def tile(t, _):
            cols = pl.ds(aligned(t, 256), 256)
            part = lax.dot_general(g_ref[rows, :], a_ref[cols, :], (((1,), (1,)), ((), ())),
                                   preferred_element_type=F32)
            p_ref[:, cols] = part
            return 0

        lax.fori_loop(0, 4, tile, 0)
        for s in range(4):
            cs_ref[j, s * 32:(s + 1) * 32, :] = p_ref[pl.ds(aligned(s * 2 + 1 - k, 32), 32), :].astype(BF16)
        send([core_copy(j)])

    def x_stage(j):
        core_copy(j).wait_recv()
        for o in range(4):
            s = (x + o) % 4
            both = (p_ref[pl.ds(aligned(s * 2 + k, 32), 32), :]
                    + cr_ref[j, pl.ds(aligned(s, 32), 32), :].astype(F32))
            if o:
                xs_ref[j, o - 1] = both.astype(BF16)
            else:
                xo_ref[j] = both
        send(x_copies(j))

    def h_stage(j):
        for copy in x_copies(j):
            copy.wait_recv()
        total = xo_ref[j]
        for o in range(3):
            total += xr_ref[j, o].astype(F32)
        if OFFS[j]:
            zs_ref[OFFS[j] - 1] = total.astype(BF16)
            send([h_copy(OFFS[j])])
        else:
            xo_ref[j] = total

    a_copy.wait()
    for j in range(4):
        z_stage(j)
    for j in range(4):
        y_stage(j)
    product_stage(0)
    x_stage(0)
    for j in range(1, 4):
        product_stage(j)
        x_stage(j)
        h_stage(j - 1)
    h_stage(3)
    total = xo_ref[OFFS.index(0)]
    for o in range(1, 4):
        h_copy(o).wait_recv()
        total += zr_ref[o - 1].astype(F32)
    share = jnp.sum(ft_ref[...].astype(F32) * total, axis=1, keepdims=True)
    wide = jnp.concatenate([jnp.broadcast_to(share, (32, 128)), jnp.zeros((96, 128), F32)], axis=0)
    dz_ref[0] = wide.T[:8]
    copies = [pltpu.make_async_remote_copy(
        dz_ref.at[0], dz_ref.at[o], ds_.at[o - 1], dr.at[o - 1],
        device_id=(row_of((zl + o) % 8, y), c), device_id_type=MESH) for o in range(1, 8)]
    send(copies)
    out_ref[...] = (-(mask_ref[...] * total)).astype(BF16)
    for copy in copies:
        copy.wait_recv()
    line = dz_ref[0]
    for o in range(1, 8):
        line += dz_ref[o]
    dy_ref[0] = line
    copies = [pltpu.make_async_remote_copy(
        dy_ref.at[0], dy_ref.at[o], es.at[o - 1], er.at[o - 1],
        device_id=(row_of(zl, (y + o) % 4), c), device_id_type=MESH) for o in range(1, 4)]
    send(copies)
    for copy in copies:
        copy.wait_recv()
    for o in range(1, 4):
        line += dy_ref[o]
    diag_ref[...] = base_ref[...] + line[0:1, 0:32]

    for here, remote in t_copies:
        pl.when(jnp.logical_not(here))(remote.wait_send)
    for copy in pending:
        copy.wait_send()


def body(factor_panel, ancestor_inverse, pattern, diag_base):
    vmem = pl.BlockSpec(memory_space=pltpu.VMEM)
    dma = pltpu.SemaphoreType.DMA
    out, diag = pl.pallas_call(
        kernel,
        out_shape=(jax.ShapeDtypeStruct((32, 1024), BF16), jax.ShapeDtypeStruct((1, 32), F32)),
        in_specs=[pl.BlockSpec(memory_space=pltpu.SMEM), vmem, vmem, pl.BlockSpec(memory_space=pl.ANY)],
        out_specs=(vmem, vmem),
        scratch_shapes=[
            pltpu.VMEM((1024, 1024), BF16),
            pltpu.VMEM((32, 1024), F32),
            pltpu.VMEM((32, 1024), BF16),
            pltpu.VMEM((1024, 1024), BF16),
            pltpu.VMEM((256, 1024), F32),
            pltpu.VMEM((4, 128, 1024), BF16),
            pltpu.VMEM((4, 128, 1024), BF16),
            pltpu.VMEM((4, 3, 32, 1024), BF16),
            pltpu.VMEM((4, 3, 32, 1024), BF16),
            pltpu.VMEM((4, 32, 1024), F32),
            pltpu.VMEM((3, 32, 1024), BF16),
            pltpu.VMEM((3, 32, 1024), BF16),
            pltpu.VMEM((8, 8, 128), F32),
            pltpu.VMEM((4, 8, 128), F32),
            dma, dma((8,)), dma((8,)), dma((12,)), dma((12,)), dma((12,)), dma((12,)),
            dma((4,)), dma((4,)), dma((12,)), dma((12,)), dma((3,)), dma((3,)),
            dma((7,)), dma((7,)), dma((3,)), dma((3,)),
        ],
        compiler_params=pltpu.CompilerParams(collective_id=0, has_side_effects=True, vmem_limit_bytes=60 << 20),
        name="selected_inverse",
    )(pattern, factor_panel.T, diag_base.reshape(1, 32), ancestor_inverse)
    return out.T, diag.reshape(32)


def solution(mesh):
    placed = (P("row", "col"), P("row", "col"), P(), P("col"))
    return jax.shard_map(
        body, mesh=mesh, in_specs=placed, out_specs=(P("row", "col"), P("col")), check_vma=False
    )
```

```python
import jax
import jax.numpy as jnp
from jax import lax
from jax.experimental import pallas as pl
from jax.experimental.pallas import tpu as pltpu
from jax.sharding import PartitionSpec as P

MESH = pl.DeviceIdType.MESH
BF16 = jnp.bfloat16
F32 = jnp.float32
ORDER = ((0, 0), (0, 1), (0, 3), (0, 2), (1, 0), (1, 1), (1, 3), (1, 2))
LANDING = (0, 1, 3, 2)
AHEAD = 3


def aligned(i, n):
    return pl.multiple_of(i * n, n)


def kernel(pattern_ref, f_ref, base_ref, a_hbm, out_ref, diag_ref,
           a_ref, mask_ref, ft_ref, g_ref, p_ref, cs_ref, cr_ref, xs_ref, xr_ref, xo_ref,
           own_ref, zs_ref, zr_ref, dz_ref, dy_ref,
           a_sem, ts, tr, zs, zr, ys, yr, cs, cr, xs, xr, hs, hr, ds_, dr, es, er):
    r, c = lax.axis_index("row"), lax.axis_index("col")
    zl, y = r // 4, r % 4
    zh, x, k = c // 8, (c // 2) % 4, c % 2
    half, q = zl // 4, zl % 4

    def row_of(zl_, y_):
        return zl_ * 4 + y_

    def col_of(zh_, x_, k_):
        return (zh_ * 4 + x_) * 2 + k_

    barrier = pltpu.get_barrier_semaphore()

    def greet(dev):
        pl.semaphore_signal(barrier, inc=1, device_id=dev, device_id_type=MESH)

    a_copy = pltpu.make_async_copy(a_hbm, a_ref, a_sem)
    a_copy.start()
    for i in range(8):
        src_col = (i // 2 * 4 + y) * 2 + i % 2
        pl.when(jnp.logical_or(c != r, src_col != c))(lambda s=src_col: greet((c, s)))
    for o in range(1, 4):
        greet((r, col_of((zh + o) % 4, x, k)))
    for o in range(1, 8):
        greet((row_of((zl + o) % 8, y), c))
    for o in range(1, 4):
        greet((row_of(zl, (y + o) % 4), c))
        greet((r, col_of(zh, (x + o) % 4, k)))
    greet((r, col_of(zh, x, 1 - k)))

    for b in range(8):
        m = pattern_ref[r * 8 + b].astype(F32)
        mask_ref[:, b * 128:(b + 1) * 128] = jnp.full((32, 128), m, F32)
    ft_ref[...] = (f_ref[...].astype(F32) * mask_ref[...]).astype(BF16)

    self_t = jnp.logical_and(c == r, row_of(zl, x) == r)
    pl.semaphore_wait(barrier, 25 - self_t.astype(jnp.int32))

    pending = []
    q_lanes = pl.ds(aligned(q, 256), 256)
    t_rows = pl.ds(aligned(x * 2 + k, 16), 16)
    own_rows = pl.ds(aligned(y, 32), 32)

    def t_copies(b):
        src = pl.ds(b * 16, 16)
        sem = (b * 4 + zh) * 2 + k
        for h in range(2):
            for p in range(4):
                lanes = pl.ds(p * 256, 256)
                there = row_of(h * 4 + p, x)
                here = jnp.logical_and(c == r, there == r)
                remote = pltpu.make_async_remote_copy(
                    ft_ref.at[src, lanes], g_ref.at[b, zh, t_rows, lanes], ts.at[b * 8 + h * 4 + p], tr.at[sem],
                    device_id=(there, r), device_id_type=MESH)
                local = pltpu.make_async_copy(
                    ft_ref.at[src, lanes], g_ref.at[b, zh, t_rows, lanes], tr.at[sem])
                yield here, remote, local

    def t_start(b):
        for here, remote, local in t_copies(b):
            pl.when(jnp.logical_not(here))(remote.start)
            pl.when(here)(local.start)

    def t_sent(b):
        for here, remote, _ in t_copies(b):
            pl.when(jnp.logical_not(here))(remote.wait_send)

    def z_copies(b, w):
        part = g_ref.at[b, w, own_rows, q_lanes]
        at = b * 12 + w * 3 - 1
        return [pltpu.make_async_remote_copy(
            part, part, zs.at[at + d], zr.at[at + d],
            device_id=(row_of(half * 4 + (q + d) % 4, y), c), device_id_type=MESH) for d in range(1, 4)]

    def y_copies(b, w):
        part = g_ref.at[b, w, own_rows, :]
        at = b * 12 + w * 3 - 1
        return [pltpu.make_async_remote_copy(
            part, part, ys.at[at + d], yr.at[at + d],
            device_id=(row_of(zl, (y + d) % 4), c), device_id_type=MESH) for d in range(1, 4)]

    def core_copy(n):
        return pltpu.make_async_remote_copy(
            cs_ref.at[n], cr_ref.at[n], cs.at[n], cr.at[n],
            device_id=(r, col_of(zh, x, 1 - k)), device_id_type=MESH)

    def x_copies(n):
        return [pltpu.make_async_remote_copy(
            xs_ref.at[n, d - 1], xr_ref.at[n, d - 1], xs.at[n * 3 + d - 1], xr.at[n * 3 + d - 1],
            device_id=(r, col_of(zh, (x + d) % 4, k)), device_id_type=MESH) for d in range(1, 4)]

    def h_copy(b, w):
        return pltpu.make_async_remote_copy(
            zs_ref.at[b, w], zr_ref.at[b, zh], hs.at[b * 4 + w], hr.at[b * 4 + zh],
            device_id=(r, col_of(w, x, k)), device_id_type=MESH)

    def h_landed(b, w):
        return pltpu.make_async_copy(zr_ref.at[b, w], zr_ref.at[b, w], hr.at[b * 4 + w])

    def send(copies):
        for copy in copies:
            copy.start()
            pending.append(copy)

    def z_stage(b, w):
        for kk in range(2):
            part = g_ref.at[b, w, pl.ds(aligned(y * 2 + kk, 16), 16), q_lanes]
            pltpu.make_async_copy(part, part, tr.at[(b * 4 + w) * 2 + kk]).wait()
        send(z_copies(b, w))

    def y_stage(n):
        b, w = ORDER[n]
        for copy in z_copies(b, w):
            copy.wait_recv()
        send(y_copies(b, w))

    def product_stage(n):
        b, w = ORDER[n]
        for copy in y_copies(b, w):
            copy.wait_recv()
        if n + AHEAD < 8:
            y_stage(n + AHEAD)

        def tile(t, _):
            cols = pl.ds(aligned(t, 256), 256)
            p_ref[n % 2, :, cols] = lax.dot_general(
                g_ref[b, w], a_ref[cols, :], (((1,), (1,)), ((), ())), preferred_element_type=F32)
            return 0

        lax.fori_loop(0, 4, tile, 0)
        for s in range(4):
            cs_ref[n, s * 16:(s + 1) * 16, :] = p_ref[n % 2, pl.ds(aligned(s * 2 + 1 - k, 16), 16), :].astype(BF16)
        send([core_copy(n)])

    def x_stage(n):
        core_copy(n).wait_recv()
        for d in range(4):
            s = (x + d) % 4
            both = (p_ref[n % 2, pl.ds(aligned(s * 2 + k, 16), 16), :]
                    + cr_ref[n, pl.ds(aligned(s, 16), 16), :].astype(F32))
            if d:
                xs_ref[n, d - 1] = both.astype(BF16)
            else:
                xo_ref[n] = both
        send(x_copies(n))

    def h_stage(n):
        b, w = ORDER[n]
        for copy in x_copies(n):
            copy.wait_recv()
        total = xo_ref[n]
        for d in range(3):
            total += xr_ref[n, d].astype(F32)

        @pl.when(zh == w)
        def _():
            own_ref[b] = total

        @pl.when(zh != w)
        def _():
            zs_ref[b, w] = total.astype(BF16)
            h_copy(b, w).start()

    for b in range(2):
        t_start(b)
    for w in LANDING:
        z_stage(0, w)
    a_copy.wait()
    for n in range(AHEAD):
        y_stage(n)
    for w in LANDING:
        z_stage(1, w)
    for n in range(10):
        if n < 8:
            product_stage(n)
        if 1 <= n < 9:
            x_stage(n - 1)
        if n >= 2:
            h_stage(n - 2)

    totals = []
    for b in range(2):
        zr_ref[b, zh] = jnp.zeros((16, 1024), BF16)
        for w in range(4):
            pl.when(zh != w)(h_landed(b, w).wait)
        total = own_ref[b]
        for w in range(4):
            total += zr_ref[b, w].astype(F32)
        totals.append(total)
    total = jnp.concatenate(totals, axis=0)
    share = jnp.sum(ft_ref[...].astype(F32) * total, axis=1, keepdims=True)
    wide = jnp.concatenate([jnp.broadcast_to(share, (32, 128)), jnp.zeros((96, 128), F32)], axis=0)
    dz_ref[0] = wide.T[:1]
    copies = [pltpu.make_async_remote_copy(
        dz_ref.at[0], dz_ref.at[o], ds_.at[o - 1], dr.at[o - 1],
        device_id=(row_of((zl + o) % 8, y), c), device_id_type=MESH) for o in range(1, 8)]
    send(copies)
    out_ref[...] = (-(mask_ref[...] * total)).astype(BF16)
    for copy in copies:
        copy.wait_recv()
    line = dz_ref[0]
    for o in range(1, 8):
        line += dz_ref[o]
    dy_ref[0] = line
    copies = [pltpu.make_async_remote_copy(
        dy_ref.at[0], dy_ref.at[o], es.at[o - 1], er.at[o - 1],
        device_id=(row_of(zl, (y + o) % 4), c), device_id_type=MESH) for o in range(1, 4)]
    send(copies)
    for copy in copies:
        copy.wait_recv()
    for o in range(1, 4):
        line += dy_ref[o]
    diag_ref[...] = base_ref[...] + line[:, 0:32]

    for b in range(2):
        t_sent(b)
        for w in range(4):
            pl.when(zh != w)(h_copy(b, w).wait_send)
    for copy in pending:
        copy.wait_send()


def body(factor_panel, ancestor_inverse, pattern, diag_base):
    vmem = pl.BlockSpec(memory_space=pltpu.VMEM)
    dma = pltpu.SemaphoreType.DMA
    out, diag = pl.pallas_call(
        kernel,
        out_shape=(jax.ShapeDtypeStruct((32, 1024), BF16), jax.ShapeDtypeStruct((1, 32), F32)),
        in_specs=[pl.BlockSpec(memory_space=pltpu.SMEM), vmem, vmem, pl.BlockSpec(memory_space=pl.ANY)],
        out_specs=(vmem, vmem),
        scratch_shapes=[
            pltpu.VMEM((1024, 1024), BF16),
            pltpu.VMEM((32, 1024), F32),
            pltpu.VMEM((32, 1024), BF16),
            pltpu.VMEM((2, 4, 128, 1024), BF16),
            pltpu.VMEM((2, 128, 1024), F32),
            pltpu.VMEM((8, 64, 1024), BF16),
            pltpu.VMEM((8, 64, 1024), BF16),
            pltpu.VMEM((8, 3, 16, 1024), BF16),
            pltpu.VMEM((8, 3, 16, 1024), BF16),
            pltpu.VMEM((8, 16, 1024), F32),
            pltpu.VMEM((2, 16, 1024), F32),
            pltpu.VMEM((2, 4, 16, 1024), BF16),
            pltpu.VMEM((2, 4, 16, 1024), BF16),
            pltpu.VMEM((8, 1, 128), F32),
            pltpu.VMEM((4, 1, 128), F32),
            dma, dma((16,)), dma((16,)), dma((24,)), dma((24,)), dma((24,)), dma((24,)),
            dma((8,)), dma((8,)), dma((24,)), dma((24,)), dma((8,)), dma((8,)),
            dma((7,)), dma((7,)), dma((3,)), dma((3,)),
        ],
        compiler_params=pltpu.CompilerParams(collective_id=0, has_side_effects=True, vmem_limit_bytes=60 << 20),
        name="selected_inverse",
    )(pattern, factor_panel.T, diag_base.reshape(1, 32), ancestor_inverse)
    return out.T, diag.reshape(32)


def solution(mesh):
    placed = (P("row", "col"), P("row", "col"), P(), P("col"))
    return jax.shard_map(
        body, mesh=mesh, in_specs=placed, out_specs=(P("row", "col"), P("col")), check_vma=False
    )
```

```python
import jax
import jax.numpy as jnp
from jax import lax
from jax.experimental import pallas as pl
from jax.experimental.pallas import tpu as pltpu
from jax.sharding import PartitionSpec as P

MESH = pl.DeviceIdType.MESH
BF16 = jnp.bfloat16
F32 = jnp.float32
ORDER = ((0, 0), (0, 1), (0, 3), (0, 2), (1, 0), (1, 1), (1, 3), (1, 2))
LANDING = (0, 1, 3, 2)
AHEAD = 3


def aligned(i, n):
    return pl.multiple_of(i * n, n)


def kernel(pattern_ref, f_ref, base_ref, a_hbm, out_ref, diag_ref,
           a_ref, mask_ref, ft_ref, g_ref, p_ref, cs_ref, cr_ref, xs_ref, xr_ref, xo_ref,
           own_ref, zs_ref, zr_ref, dz_ref,
           a_sem, ts, tr, zs, zr, ys, yr, cs, cr, xs, xr, hs, hr, ds_, dr):
    r, c = lax.axis_index("row"), lax.axis_index("col")
    zl, y = r // 4, r % 4
    zh, x, k = c // 8, (c // 2) % 4, c % 2
    half, q = zl // 4, zl % 4

    def row_of(zl_, y_):
        return zl_ * 4 + y_

    def col_of(zh_, x_, k_):
        return (zh_ * 4 + x_) * 2 + k_

    barrier = pltpu.get_barrier_semaphore()

    def greet(dev):
        pl.semaphore_signal(barrier, inc=1, device_id=dev, device_id_type=MESH)

    a_copy = pltpu.make_async_copy(a_hbm, a_ref, a_sem)
    a_copy.start()
    for i in range(8):
        src_col = (i // 2 * 4 + y) * 2 + i % 2
        pl.when(jnp.logical_or(c != r, src_col != c))(lambda s=src_col: greet((c, s)))
    for o in range(1, 4):
        greet((r, col_of((zh + o) % 4, x, k)))
    for o in range(1, 4):
        greet((r, col_of(zh, (x + o) % 4, k)))
    greet((r, col_of(zh, x, 1 - k)))

    def each_row_peer(act):
        def step(o, _):
            act((r + o) % 32)
            return 0
        lax.fori_loop(1, 32, step, 0)

    each_row_peer(lambda peer: greet((peer, c)))

    for b in range(8):
        m = pattern_ref[r * 8 + b].astype(F32)
        mask_ref[:, b * 128:(b + 1) * 128] = jnp.full((32, 128), m, F32)
    ft_ref[...] = (f_ref[...].astype(F32) * mask_ref[...]).astype(BF16)

    self_t = jnp.logical_and(c == r, row_of(zl, x) == r)
    pl.semaphore_wait(barrier, 46 - self_t.astype(jnp.int32))

    pending = []
    q_lanes = pl.ds(aligned(q, 256), 256)
    t_rows = pl.ds(aligned(x * 2 + k, 16), 16)
    own_rows = pl.ds(aligned(y, 32), 32)

    def t_copies(b):
        src = pl.ds(b * 16, 16)
        sem = (b * 4 + zh) * 2 + k
        for h in range(2):
            for p in range(4):
                lanes = pl.ds(p * 256, 256)
                there = row_of(h * 4 + p, x)
                here = jnp.logical_and(c == r, there == r)
                remote = pltpu.make_async_remote_copy(
                    ft_ref.at[src, lanes], g_ref.at[b, zh, t_rows, lanes], ts.at[b * 8 + h * 4 + p], tr.at[sem],
                    device_id=(there, r), device_id_type=MESH)
                local = pltpu.make_async_copy(
                    ft_ref.at[src, lanes], g_ref.at[b, zh, t_rows, lanes], tr.at[sem])
                yield here, remote, local

    def t_start(b):
        for here, remote, local in t_copies(b):
            pl.when(jnp.logical_not(here))(remote.start)
            pl.when(here)(local.start)

    def t_sent(b):
        for here, remote, _ in t_copies(b):
            pl.when(jnp.logical_not(here))(remote.wait_send)

    def z_copies(b, w):
        part = g_ref.at[b, w, own_rows, q_lanes]
        at = b * 12 + w * 3 - 1
        return [pltpu.make_async_remote_copy(
            part, part, zs.at[at + d], zr.at[at + d],
            device_id=(row_of(half * 4 + (q + d) % 4, y), c), device_id_type=MESH) for d in range(1, 4)]

    def y_copies(b, w):
        part = g_ref.at[b, w, own_rows, :]
        at = b * 12 + w * 3 - 1
        return [pltpu.make_async_remote_copy(
            part, part, ys.at[at + d], yr.at[at + d],
            device_id=(row_of(zl, (y + d) % 4), c), device_id_type=MESH) for d in range(1, 4)]

    def core_copy(n):
        return pltpu.make_async_remote_copy(
            cs_ref.at[n], cr_ref.at[n], cs.at[n], cr.at[n],
            device_id=(r, col_of(zh, x, 1 - k)), device_id_type=MESH)

    def x_copies(n):
        return [pltpu.make_async_remote_copy(
            xs_ref.at[n, d - 1], xr_ref.at[n, d - 1], xs.at[n * 3 + d - 1], xr.at[n * 3 + d - 1],
            device_id=(r, col_of(zh, (x + d) % 4, k)), device_id_type=MESH) for d in range(1, 4)]

    def h_copy(b, w):
        return pltpu.make_async_remote_copy(
            zs_ref.at[b, w], zr_ref.at[b, zh], hs.at[b * 4 + w], hr.at[b * 4 + zh],
            device_id=(r, col_of(w, x, k)), device_id_type=MESH)

    def h_landed(b, w):
        return pltpu.make_async_copy(zr_ref.at[b, w], zr_ref.at[b, w], hr.at[b * 4 + w])

    def send(copies):
        for copy in copies:
            copy.start()
            pending.append(copy)

    def z_stage(b, w):
        for kk in range(2):
            part = g_ref.at[b, w, pl.ds(aligned(y * 2 + kk, 16), 16), q_lanes]
            pltpu.make_async_copy(part, part, tr.at[(b * 4 + w) * 2 + kk]).wait()
        send(z_copies(b, w))

    def y_stage(n):
        b, w = ORDER[n]
        for copy in z_copies(b, w):
            copy.wait_recv()
        send(y_copies(b, w))

    def product_stage(n):
        b, w = ORDER[n]
        for copy in y_copies(b, w):
            copy.wait_recv()
        if n + AHEAD < 8:
            y_stage(n + AHEAD)

        def tile(t, _):
            cols = pl.ds(aligned(t, 256), 256)
            p_ref[n % 2, :, cols] = lax.dot_general(
                g_ref[b, w], a_ref[cols, :], (((1,), (1,)), ((), ())), preferred_element_type=F32)
            return 0

        lax.fori_loop(0, 4, tile, 0)
        for s in range(4):
            cs_ref[n, s * 16:(s + 1) * 16, :] = p_ref[n % 2, pl.ds(aligned(s * 2 + 1 - k, 16), 16), :].astype(BF16)
        send([core_copy(n)])

    def x_stage(n):
        core_copy(n).wait_recv()
        for d in range(4):
            s = (x + d) % 4
            both = (p_ref[n % 2, pl.ds(aligned(s * 2 + k, 16), 16), :]
                    + cr_ref[n, pl.ds(aligned(s, 16), 16), :].astype(F32))
            if d:
                xs_ref[n, d - 1] = both.astype(BF16)
            else:
                xo_ref[n] = both
        send(x_copies(n))

    def h_stage(n):
        b, w = ORDER[n]
        for copy in x_copies(n):
            copy.wait_recv()
        total = xo_ref[n]
        for d in range(3):
            total += xr_ref[n, d].astype(F32)

        @pl.when(zh == w)
        def _():
            own_ref[b] = total

        @pl.when(zh != w)
        def _():
            zs_ref[b, w] = total.astype(BF16)
            h_copy(b, w).start()

    for b in range(2):
        t_start(b)
    for w in LANDING:
        z_stage(0, w)
    a_copy.wait()
    for n in range(AHEAD):
        y_stage(n)
    for w in LANDING:
        z_stage(1, w)
    for n in range(10):
        if n < 8:
            product_stage(n)
        if 1 <= n < 9:
            x_stage(n - 1)
        if n >= 2:
            h_stage(n - 2)

    totals = []
    for b in range(2):
        zr_ref[b, zh] = jnp.zeros((16, 1024), BF16)
        for w in range(4):
            pl.when(zh != w)(h_landed(b, w).wait)
        total = own_ref[b]
        for w in range(4):
            total += zr_ref[b, w].astype(F32)
        totals.append(total)
    total = jnp.concatenate(totals, axis=0)
    share = jnp.sum(ft_ref[...].astype(F32) * total, axis=1, keepdims=True)
    wide = jnp.concatenate([jnp.broadcast_to(share, (32, 128)), jnp.zeros((96, 128), F32)], axis=0)
    dz_ref[r] = wide.T[:1]

    def share_copy(peer):
        return pltpu.make_async_remote_copy(
            dz_ref.at[r], dz_ref.at[r], ds_.at[peer], dr.at[r], device_id=(peer, c), device_id_type=MESH)

    def share_landed(peer):
        return pltpu.make_async_copy(dz_ref.at[peer], dz_ref.at[peer], dr.at[peer])

    each_row_peer(lambda peer: share_copy(peer).start())
    out_ref[...] = (-(mask_ref[...] * total)).astype(BF16)
    each_row_peer(lambda peer: share_landed(peer).wait())
    diag_ref[...] = base_ref[...] + jnp.sum(dz_ref[...], axis=0)[:, 0:32]

    each_row_peer(lambda peer: share_copy(peer).wait_send())
    for b in range(2):
        t_sent(b)
        for w in range(4):
            pl.when(zh != w)(h_copy(b, w).wait_send)
    for copy in pending:
        copy.wait_send()


def body(factor_panel, ancestor_inverse, pattern, diag_base):
    vmem = pl.BlockSpec(memory_space=pltpu.VMEM)
    dma = pltpu.SemaphoreType.DMA
    out, diag = pl.pallas_call(
        kernel,
        out_shape=(jax.ShapeDtypeStruct((32, 1024), BF16), jax.ShapeDtypeStruct((1, 32), F32)),
        in_specs=[pl.BlockSpec(memory_space=pltpu.SMEM), vmem, vmem, pl.BlockSpec(memory_space=pl.ANY)],
        out_specs=(vmem, vmem),
        scratch_shapes=[
            pltpu.VMEM((1024, 1024), BF16),
            pltpu.VMEM((32, 1024), F32),
            pltpu.VMEM((32, 1024), BF16),
            pltpu.VMEM((2, 4, 128, 1024), BF16),
            pltpu.VMEM((2, 128, 1024), F32),
            pltpu.VMEM((8, 64, 1024), BF16),
            pltpu.VMEM((8, 64, 1024), BF16),
            pltpu.VMEM((8, 3, 16, 1024), BF16),
            pltpu.VMEM((8, 3, 16, 1024), BF16),
            pltpu.VMEM((8, 16, 1024), F32),
            pltpu.VMEM((2, 16, 1024), F32),
            pltpu.VMEM((2, 4, 16, 1024), BF16),
            pltpu.VMEM((2, 4, 16, 1024), BF16),
            pltpu.VMEM((32, 1, 128), F32),
            dma, dma((16,)), dma((16,)), dma((24,)), dma((24,)), dma((24,)), dma((24,)),
            dma((8,)), dma((8,)), dma((24,)), dma((24,)), dma((8,)), dma((8,)),
            dma((32,)), dma((32,)),
        ],
        compiler_params=pltpu.CompilerParams(collective_id=0, has_side_effects=True, vmem_limit_bytes=60 << 20),
        name="selected_inverse",
    )(pattern, factor_panel.T, diag_base.reshape(1, 32), ancestor_inverse)
    return out.T, diag.reshape(32)


def solution(mesh):
    placed = (P("row", "col"), P("row", "col"), P(), P("col"))
    return jax.shard_map(
        body, mesh=mesh, in_specs=placed, out_specs=(P("row", "col"), P("col")), check_vma=False
    )
```
